32 devices in a mesh: ctx: 8 (over z, y), head: 4 (over x, core).
Axes of the slice: x: 2, y: 2, z: 4, core: 2. Of those that a mesh axis runs over, the one named last changes fastest.
Arguments:
- prompt_states: bfloat16 [4096, 2048], P('ctx')
- decode_states: bfloat16 [4, 2048], replicated
- lengths: int32 [4], replicated, may hold values from 1 to 2048, 4096 in all
- page_table: int32 [32], replicated, may hold values from 0 to 31, as said below
- w_query: bfloat16 [2048, 3072], P(None, 'head'), may hold values from -0.125 to 0.125
- w_down: bfloat16 [2048, 576], replicated, may hold values from -0.125 to 0.125
- kv_gain: float32 [512], replicated, may hold values from 0.1 to 1.9
- w_up: bfloat16 [512, 4096], P(None, 'head'), may hold values from -0.25 to 0.25
- w_out: bfloat16 [2048, 2048], P('head'), may hold values from -0.125 to 0.125
Outputs:
- prefill_out: bfloat16 [4096, 2048], P(('ctx', 'head'))
- paged_cache: bfloat16 [4096, 576], P('ctx')
- decode_out: bfloat16 [4, 2048], replicated
The draws below stay inside these ranges and needn't reach their ends.
Inputs may be any that keep to these rules, and one draw needn't show every extreme that they name: page_table is a permutation of the 32 pages; the logical pages of ctx index c are c * 4 to c * 4 + 3, and physical page p lies on ctx index p // 4; logical page c * 4 + w has physical page ((c + s_w) mod 8) * 4 + w, where the shifts s_0 to s_(3) are distinct numbers of 0 to 8 - 1, the same for every c.
All inputs are finite; a program needn't handle non-finite values.
Results may differ from the reference program's by a relative error of at most 0.025.
Values may be sent and summed in bfloat16 or wider, within the bound.
A program may use at most 192 MiB of HBM per device.

```python
import math
import jax
import jax.numpy as jnp
import numpy as np
from jax import lax

D = 2048
HEADS = 16
NOPE = 128
ROPE = 64
VDIM = 128
RANK = 512
PAGE = 128
REQS = 4
TOK_DEV = 512
TOKENS = 4096
PAGES_DEV = 4
PAGES = 32
N_CTX = 8


def rough_states(key, rows):
    return jax.random.normal(key, (rows, D), jnp.float32).astype(jnp.bfloat16)


def draw_prompt_states(key, part):
    return rough_states(jax.random.fold_in(key, 11), TOKENS)


def draw_decode_states(key, part):
    return rough_states(jax.random.fold_in(key, 12), REQS)


def draw_page_table(key, part):
    offsets = jax.random.permutation(jax.random.fold_in(key, 13), N_CTX)[:PAGES_DEV]
    logical = jnp.arange(PAGES, dtype=jnp.int32)
    source = logical // PAGES_DEV
    within = logical % PAGES_DEV
    target = (source + offsets[within]) % N_CTX
    return (target * PAGES_DEV + within).astype(jnp.int32)


def levels(rng, shape, shards, least, top_value):
    level = 1.0
    for axis_at, shards_of in shards:
        draws = jax.random.uniform(jax.random.fold_in(jax.random.fold_in(rng, 6), axis_at), (shards_of,), jnp.float32, least / len(shards), top_value / len(shards))
        level = level * jnp.repeat(jnp.exp(draws), shape[axis_at] // shards_of).reshape((-1,) + (1,) * (len(shape) - 1 - axis_at))
    return level


def profile(number_of, total, most, skew):
    weights = [(1 << 20) // math.isqrt(grade ** skew) + 1 for grade in range(2, number_of + 1)]
    spare, counts = total - most - (number_of - 1), [1] * (number_of - 1)
    while spare > 0:
        free = [i for i in range(number_of - 1) if counts[i] < most]
        whole, left = sum([weights[i] for i in free]), spare
        for i in free:
            addition = min(most - counts[i], max(1, left * weights[i] // whole), spare)
            counts[i] = counts[i] + addition
            spare = spare - addition
    return np.array([most] + counts)


def uneven_parts(stream_key, number_of, total, limit, lean):
    if number_of == 2:
        one = jax.random.randint(stream_key, (), max(1, total - limit), min(limit, total - 1) + 1)
        return jnp.stack([one, total - one])
    tallies = jnp.asarray(profile(number_of, total, limit, lean), jnp.int32)
    couples = (number_of - 1) // 2
    giver, taker = tallies[1:1 + 2 * couples:2], tallies[2:2 + 2 * couples:2]
    room = jnp.minimum(giver - 1, limit - taker)
    moved = jax.random.randint(jax.random.fold_in(stream_key, 1), (couples,), 0, 1 << 20) % (room + 1)
    tallies = tallies.at[1:1 + 2 * couples:2].set(giver - moved).at[2:2 + 2 * couples:2].set(taker + moved)
    return tallies[jax.random.permutation(jax.random.fold_in(stream_key, 2), number_of)]


def noise(key, dims, spread, most, pieces=(), held_as=jnp.bfloat16):
    level = levels(key, dims, pieces, -0.22, 0.18) if pieces else 1.0
    values = jax.random.normal(key, dims, jnp.float32) * spread * level
    return jnp.minimum(jnp.maximum(values, -most), most).astype(held_as)


def setup_inputs(seed: int = 0) -> dict:
    key_of = jax.random.split(jax.random.key(seed), 10)
    return {
        "prompt_states": draw_prompt_states(jax.random.fold_in(key_of[9], 71), 0),
        "decode_states": draw_decode_states(jax.random.fold_in(key_of[9], 71), 0),
        "lengths": uneven_parts(key_of[2], REQS, TOKENS, TOKENS // 2, 2).astype(jnp.int32),
        "page_table": draw_page_table(jax.random.fold_in(key_of[9], 71), 0),
        "w_query": noise(key_of[4], (D, HEADS * (NOPE + ROPE)), D ** -0.5, 0.125, ((1, 4),)),
        "w_down": noise(key_of[5], (D, RANK + ROPE), D ** -0.5, 0.125),
        "kv_gain": jnp.clip(1.0 + 0.18 * jax.random.normal(key_of[6], (RANK,), jnp.float32), 0.1, 1.9),
        "w_up": noise(key_of[7], (RANK, HEADS * (NOPE + VDIM)), RANK ** -0.5, 0.25, ((1, 4),)),
        "w_out": noise(key_of[8], (HEADS * VDIM, D), (HEADS * VDIM) ** -0.5, 0.125, ((0, 4),)),
    }


ROPE_BASE = 50000.0

def rope(vector, place):
    half = vector.shape[-1] // 2
    freq = ROPE_BASE ** (-(jnp.arange(half, dtype=jnp.float32) * 2.0 / vector.shape[-1]))
    angle = place[..., None] * freq
    first, second = (vector[..., :half], vector[..., half:])
    return jnp.concatenate([first * jnp.cos(angle) - second * jnp.sin(angle), first * jnp.sin(angle) + second * jnp.cos(angle)], -1)

def token_info(index, lengths):
    ends = jnp.cumsum(lengths).astype(jnp.int32)
    starts = (ends - lengths).astype(jnp.int32)
    tenant = lax.optimization_barrier(jnp.sum((index[:, None] >= ends[None, :]).astype(jnp.int32), 1)).astype(jnp.int32)
    picked = lax.optimization_barrier(jnp.sum(jnp.where(tenant[:, None] == jnp.arange(lengths.shape[0], dtype=jnp.int32)[None, :], starts[None, :], 0), 1))
    return (tenant, (index - picked).astype(jnp.int32))

def latent_of(states, w_down, kv_gain, place):
    lat = jnp.dot(states, w_down, preferred_element_type=jnp.float32)
    comp = lat[:, :RANK]
    comp = comp * lax.rsqrt(lax.optimization_barrier(jnp.mean(comp * comp, -1, keepdims=True)) + 1e-06) * kv_gain
    return jnp.concatenate([comp, rope(lat[:, RANK:], place)], 1).astype(jnp.bfloat16)

def queries(states, w_query, w_up, place):
    rows = states.shape[0]
    heads = w_query.shape[1] // (NOPE + ROPE)
    qfull = jnp.dot(states, w_query, preferred_element_type=jnp.float32).astype(jnp.bfloat16).reshape(rows, heads, NOPE + ROPE)
    w_key = w_up.reshape(RANK, heads, NOPE + VDIM)[:, :, :NOPE]
    qnope = jnp.einsum('thn,rhn->thr', qfull[..., :NOPE].astype(jnp.float32), w_key.astype(jnp.float32))
    qrope = rope(qfull[..., NOPE:].astype(jnp.float32), place[:, None])
    scale = (NOPE + ROPE) ** (-0.5)
    return (jnp.concatenate([qnope, qrope], -1) * scale).astype(jnp.bfloat16)

def values_of(mixed, w_up):
    heads = w_up.shape[1] // (NOPE + VDIM)
    w_val = w_up.reshape(RANK, heads, NOPE + VDIM)[:, :, NOPE:]
    out = jnp.einsum('thr,rhv->thv', mixed.astype(jnp.float32), w_val.astype(jnp.float32))
    return out.astype(jnp.bfloat16).reshape(mixed.shape[0], heads * VDIM)

def reference(prompt_states, decode_states, lengths, page_table, w_query, w_down, kv_gain, w_up, w_out):
    index = jnp.arange(TOKENS, dtype=jnp.int32)
    tenant, place = token_info(index, lengths)
    latent = latent_of(prompt_states, w_down, kv_gain, place.astype(jnp.float32))
    query = queries(prompt_states, w_query, w_up, place.astype(jnp.float32))
    keys = latent.astype(jnp.float32)

    def block(item):
        qblock, iblock, tblock = item
        score = jnp.einsum('thk,uk->thu', qblock.astype(jnp.float32), keys)
        mask = (tenant[None, :] == tblock[:, None]) & (index[None, :] <= iblock[:, None])
        score = jnp.where(mask[:, None, :], score, -jnp.inf)
        top = lax.optimization_barrier(jnp.max(score, -1, keepdims=True))
        prob = jnp.where(mask[:, None, :], jnp.exp(score - top), 0.0)
        total = lax.optimization_barrier(jnp.sum(prob, -1))
        acc = jnp.einsum('thu,ur->thr', prob.astype(jnp.bfloat16).astype(jnp.float32), keys[:, :RANK])
        return (acc / total[..., None]).astype(jnp.bfloat16)
    mixed = lax.map(block, (query.reshape(N_CTX, TOK_DEV, HEADS, RANK + ROPE), index.reshape(N_CTX, TOK_DEV), tenant.reshape(N_CTX, TOK_DEV)))
    mixed = mixed.reshape(TOKENS, HEADS, RANK)
    heads_out = values_of(mixed, w_up)
    prefill_out = jnp.dot(heads_out, w_out, preferred_element_type=jnp.float32).astype(jnp.bfloat16)
    rows = (page_table[:, None] * PAGE + jnp.arange(PAGE, dtype=jnp.int32)[None, :]).reshape(-1).astype(jnp.int32)
    paged_cache = jnp.zeros((TOKENS, RANK + ROPE), jnp.bfloat16).at[rows].set(latent)
    dplace = lengths.astype(jnp.float32)
    new_key = latent_of(decode_states, w_down, kv_gain, dplace)
    dquery = queries(decode_states, w_query, w_up, dplace).astype(jnp.float32)
    score = jnp.einsum('qhk,uk->qhu', dquery, keys)
    dmask = tenant[None, :] == jnp.arange(REQS, dtype=jnp.int32)[:, None]
    score = jnp.where(dmask[:, None, :], score, -jnp.inf)
    own = jnp.einsum('qhk,qk->qh', dquery, new_key.astype(jnp.float32))
    top = jnp.maximum(lax.optimization_barrier(jnp.max(score, -1)), own)
    prob = jnp.where(dmask[:, None, :], jnp.exp(score - top[..., None]), 0.0)
    pown = jnp.exp(own - top)
    total = lax.optimization_barrier(jnp.sum(prob, -1)) + pown
    acc = jnp.einsum('qhu,ur->qhr', prob.astype(jnp.bfloat16).astype(jnp.float32), keys[:, :RANK])
    acc = acc + pown.astype(jnp.bfloat16).astype(jnp.float32)[..., None] * new_key[:, None, :RANK].astype(jnp.float32)
    dmixed = (acc / total[..., None]).astype(jnp.bfloat16)
    dheads = values_of(dmixed, w_up)
    decode_out = jnp.dot(dheads, w_out, preferred_element_type=jnp.float32).astype(jnp.bfloat16)
    return (prefill_out, paged_cache, decode_out)
```

```python
import functools
import math

import jax
import jax.numpy as jnp
from jax import lax
from jax.experimental import pallas as pl
from jax.experimental.pallas import tpu as pltpu
from jax.sharding import PartitionSpec as P

NOPE = 128
ROPE = 64
VDIM = 128
RANK = 512
PAGE = 128
WIDTH = RANK + ROPE
QK = NOPE + ROPE
ROPE_BASE = 50000.0
NEG = -1e30
SCALE = QK ** (-0.5) * math.log2(math.e)
MESH = pl.DeviceIdType.MESH
LINE = 4


def trig(place, size):
    half = size // 2
    freq = ROPE_BASE ** (-(jnp.arange(half, dtype=jnp.float32) * 2.0 / size))
    angle = place[..., None] * freq
    return jnp.cos(angle), jnp.sin(angle)


def turn(vector, cos, sin):
    half = vector.shape[-1] // 2
    first, second = vector[..., :half], vector[..., half:]
    return jnp.concatenate([first * cos - second * sin, first * sin + second * cos], -1)


def latent_of(states, w_down, kv_gain, cos, sin):
    lat = jnp.dot(states, w_down, preferred_element_type=jnp.float32)
    comp = lat[:, :RANK]
    comp = comp * lax.rsqrt(jnp.mean(comp * comp, -1, keepdims=True) + 1e-06) * kv_gain
    return jnp.concatenate([comp, turn(lat[:, RANK:], cos, sin)], 1).astype(jnp.bfloat16)


def kernel(
    n_ctx, n_head, heads, q_ref, lat_ref, start_ref, dq_ref, dtop_ref, dacc_ref, dlow_ref, dhigh_ref,
    shift_ref, w_up_ref, w_out_ref, out_ref, cache_ref, dec_ref,
    got, kbuf, vbuf, acc, top, ho, sib_out, sib_in, far_out, far_in, near_out, near_in,
    dsib_out, dsib_in, dfar, send_sems, recv_sems, core_sems, sum_send, sum_recv,
):
    tok = lat_ref.shape[0]
    half = tok // 2
    line_b = n_ctx // LINE
    window = n_ctx // 2
    c = lax.axis_index("ctx")
    m = lax.axis_index("head")
    a, b = c // line_b, c % line_b
    x, k = m // 2, m % 2
    sib = x * 2 + 1 - k
    n_x = n_head // 2
    fars = [lax.rem(x + r, n_x) for r in range(1, n_x)]
    up_a, dn_a, up_b, dn_b = a < LINE - 1, a > 0, b < line_b - 1, b > 0
    moves = [(up_a, line_b), (dn_a, -line_b), (up_b, 1), (dn_b, -1)]

    barrier = pltpu.get_barrier_semaphore()
    for ok, step in moves:
        @pl.when(ok)
        def _(step=step):
            pl.semaphore_signal(barrier, inc=1, device_id=(c + step, m), device_id_type=MESH)
    for other in [sib] + [xo * 2 + k for xo in fars]:
        pl.semaphore_signal(barrier, inc=1, device_id=(c, other), device_id_type=MESH)
    peers = jnp.minimum(a, 1) + jnp.minimum(LINE - 1 - a, 1)
    peers = peers + jnp.minimum(b, 1) + jnp.minimum(line_b - 1 - b, 1)
    pl.semaphore_wait(barrier, peers + n_x)

    def hop(blk, way):
        return pltpu.make_async_remote_copy(
            src_ref=got.at[blk, k], dst_ref=got.at[blk, k], send_sem=send_sems.at[way, blk],
            recv_sem=recv_sems.at[blk], device_id=(c + moves[way][1], m), device_id_type=MESH)

    def across(blk, side):
        return pltpu.make_async_remote_copy(
            src_ref=got.at[blk, side], dst_ref=got.at[blk, side], send_sem=send_sems.at[4, blk],
            recv_sem=core_sems.at[blk], device_id=(c, sib), device_id_type=MESH)

    sent = []

    def send(ok, blk, way):
        @pl.when(ok)
        def _():
            (hop(blk, way) if way < 4 else across(blk, k)).start()
        sent.append((ok, blk, way))

    got[c] = lat_ref[...].reshape(2, half, WIDTH)
    for way in range(4):
        send(moves[way][0], c, way)

    far_step = LINE - 1 + line_b - 1
    stages = [[] for _ in range(far_step + 1)]
    for i in range(-(LINE - 1), LINE):
        for j in range(-(line_b - 1), line_b):
            if (i, j) != (0, 0):
                stages[abs(i) + abs(j)].append((i, j))

    def where_from(i, j):
        ok = jnp.logical_and(jnp.logical_and(a + i >= 0, a + i < LINE),
                             jnp.logical_and(b + j >= 0, b + j < line_b))
        blk = lax.rem(c + i * line_b + j + n_ctx * 2, n_ctx)
        return ok, blk

    def arrive(step):
        for i, j in stages[step]:
            ok, blk = where_from(i, j)

            @pl.when(ok)
            def _(blk=blk):
                hop(blk, 0).wait_recv()
            if j == 0:
                way = 0 if i < 0 else 1
                send(jnp.logical_and(ok, moves[way][0]), blk, way)
                send(jnp.logical_and(ok, up_b), blk, 2)
                send(jnp.logical_and(ok, dn_b), blk, 3)
            else:
                way = 2 if j < 0 else 3
                send(jnp.logical_and(ok, moves[way][0]), blk, way)
            send(ok, blk, 4)

    def settle(step):
        for i, j in stages[step]:
            ok, blk = where_from(i, j)

            @pl.when(ok)
            def _(blk=blk):
                across(blk, 1 - k).wait_recv()

    vbuf[:, :, VDIM:] = jnp.ones((heads, tok, VDIM), jnp.bfloat16)

    def attend(d):
        src = jnp.maximum(c - d, 0)
        for h in range(heads):
            part = jnp.dot(got[src, :, :, :RANK].reshape(tok, RANK),
                           w_up_ref[:, h * 256:(h + 1) * 256], preferred_element_type=jnp.float32)
            part = part.astype(jnp.bfloat16)
            kbuf[h, :, :NOPE] = part[:, :NOPE]
            kbuf[h, :, NOPE:] = got[src, :, :, RANK:].reshape(tok, ROPE)
            vbuf[h, :, :VDIM] = part[:, NOPE:]

        def head(h, carry):
            s = lax.dot_general(q_ref[h], kbuf[h], (((1,), (1,)), ((), ())),
                                preferred_element_type=jnp.float32)
            key = src * tok + lax.broadcasted_iota(jnp.int32, (tok, tok), 1)
            ok = key >= start_ref[...]
            if d == 0:
                row = c * tok + lax.broadcasted_iota(jnp.int32, (tok, tok), 0)
                ok = jnp.logical_and(ok, key <= row)
            s = jnp.where(ok, s, NEG)
            best = jnp.max(s, axis=1, keepdims=True)
            if d > 0:
                old = top[h][:, :1]
                best = jnp.maximum(old, best)
            p = jnp.exp2(s - best).astype(jnp.bfloat16)
            pv = jnp.dot(p, vbuf[h], preferred_element_type=jnp.float32)
            if d > 0:
                pv = pv + acc[h] * jnp.exp2(old - best)
            acc[h] = pv
            top[h] = jnp.broadcast_to(best, (tok, 128))
            return carry

        lax.fori_loop(0, heads, head, 0)

    def attend_if(d):
        if d <= window:
            @pl.when(c >= d)
            def _():
                attend(d)

    attend(0)
    if line_b == 2:
        arrive(1)
        settle(1)
        attend_if(2)
        arrive(2)
        settle(2)
        attend_if(1)
        attend_if(4)
        arrive(3)
        settle(3)
        attend_if(3)
        arrive(4)
    else:
        for step in range(1, far_step + 1):
            arrive(step)
            if step < far_step:
                settle(step)
        settle(far_step)
        for d in range(1, window + 1):
            attend_if(d)

    for h in range(heads):
        ho[:, h * VDIM:(h + 1) * VDIM] = (acc[h, :, :VDIM] / acc[h, :, VDIM:]).astype(jnp.bfloat16)
    rows = tok // n_head

    def project(group):
        return jnp.dot(ho[pl.ds(pl.multiple_of(group * rows, rows), rows), :], w_out_ref[...],
                       preferred_element_type=jnp.float32)

    def swap(src, dst, number, other):
        return pltpu.make_async_remote_copy(
            src_ref=src, dst_ref=dst, send_sem=sum_send.at[number], recv_sem=sum_recv.at[number],
            device_id=(c, other), device_id_type=MESH)

    turns = range(n_x - 1)
    first = [swap(sib_out.at[r], sib_in.at[r], r, sib) for r in turns]
    second = [swap(far_out.at[r], far_in.at[r], n_x + r, fars[r] * 2 + k) for r in turns]
    third = swap(near_out, near_in, n_x - 1, sib)
    fourth = swap(dsib_out, dsib_in, 2 * n_x - 1, sib)
    fifth = [swap(dfar.at[x], dfar.at[x], 2 * n_x + r, fars[r] * 2 + k) for r in turns]
    for r in turns:
        sib_out[r] = project(fars[r] * 2 + 1 - k).astype(jnp.bfloat16)
        first[r].start()
    for r in turns:
        mine = project(fars[r] * 2 + k)
        first[r].wait_recv()
        far_out[r] = (mine + sib_in[r].astype(jnp.float32)).astype(jnp.bfloat16)
        second[r].start()
    near_out[...] = project(sib).astype(jnp.bfloat16)
    third.start()
    if line_b == 2:
        settle(far_step)

    def decode(j, carry):
        best, total, mix = carry
        keys = got[j].reshape(tok, WIDTH)
        s = lax.dot_general(dq_ref[...], keys, (((1,), (1,)), ((), ())),
                            preferred_element_type=jnp.float32)
        key = j * tok + lax.broadcasted_iota(jnp.int32, s.shape, 1)
        ok = jnp.logical_and(key >= dlow_ref[...], key < dhigh_ref[...])
        s = jnp.where(ok, s, NEG)
        new = jnp.maximum(best, jnp.max(s, axis=1, keepdims=True))
        p = jnp.exp2(s - new)
        ratio = jnp.exp2(best - new)
        total = total * ratio + jnp.sum(p, axis=1, keepdims=True)
        mix = mix * ratio + jnp.dot(p.astype(jnp.bfloat16), keys[:, :RANK],
                                    preferred_element_type=jnp.float32)
        return new, total, mix

    drows = dq_ref.shape[0] // heads
    _, total, mix = lax.fori_loop(
        0, n_ctx, decode, (dtop_ref[...], jnp.ones(dtop_ref.shape, jnp.float32), dacc_ref[...]))
    mix = (mix / total).astype(jnp.bfloat16)
    dheads = [jnp.dot(mix, w_up_ref[:, h * 256 + NOPE:(h + 1) * 256],
                      preferred_element_type=jnp.float32)[h * drows:(h + 1) * drows]
              for h in range(heads)]
    dheads = jnp.concatenate(dheads, 1).astype(jnp.bfloat16)
    dsib_out[...] = jnp.dot(dheads, w_out_ref[...], preferred_element_type=jnp.float32)
    fourth.start()
    for w in range(tok // PAGE):
        blk = lax.rem(c - shift_ref[w] + n_ctx, n_ctx)
        part = got[blk, w * PAGE // half, (w * PAGE) % half:(w * PAGE) % half + PAGE, :]
        cache_ref[w * PAGE:(w + 1) * PAGE, :] = part
    fourth.wait_recv()
    dfar[x] = dsib_out[...] + dsib_in[...]
    for copy in fifth:
        copy.start()
    mine = project(m)
    third.wait_recv()
    mine = mine + near_in[...].astype(jnp.float32)
    for r in turns:
        second[r].wait_recv()
        mine = mine + far_in[r].astype(jnp.float32)
    out_ref[...] = mine.astype(jnp.bfloat16)
    for r in turns:
        source = lax.rem(x - 1 - r + n_x, n_x)
        swap(dfar.at[source], dfar.at[source], 2 * n_x + r, fars[r] * 2 + k).wait_recv()
    dec = dfar[0]
    for xo in range(1, n_x):
        dec = dec + dfar[xo]
    dec_ref[...] = dec.astype(jnp.bfloat16)
    for copy in first + second + [third, fourth] + fifth:
        copy.wait_send()
    for ok, blk, way in sent:
        @pl.when(ok)
        def _(blk=blk, way=way):
            (hop(blk, way) if way < 4 else across(blk, k)).wait_send()


def on_device(
    n_ctx, n_head, prompt_states, decode_states, lengths, page_table, w_query, w_down, kv_gain, w_up, w_out
):
    tok = prompt_states.shape[0]
    heads = w_query.shape[1] // QK
    width = w_out.shape[1]
    requests = decode_states.shape[0]
    c = lax.axis_index("ctx")
    ends = jnp.cumsum(lengths)
    starts = ends - lengths
    index = c * tok + jnp.arange(tok, dtype=jnp.int32)
    start = jnp.max(jnp.where(index[:, None] >= starts[None, :], starts[None, :], 0), 1)
    cos, sin = trig((index - start).astype(jnp.float32), ROPE)
    latent = latent_of(prompt_states, w_down, kv_gain, cos, sin)
    q = jnp.dot(prompt_states, w_query, preferred_element_type=jnp.float32)
    q = q.reshape(tok, heads, QK).transpose(1, 0, 2)
    q = (jnp.concatenate([q[..., :NOPE], turn(q[..., NOPE:], cos, sin)], -1) * SCALE).astype(
        jnp.bfloat16)

    dcos, dsin = trig(lengths.astype(jnp.float32), ROPE)
    new_key = latent_of(decode_states, w_down, kv_gain, dcos, dsin)
    dq = jnp.dot(decode_states, w_query, preferred_element_type=jnp.float32)
    dq = dq.astype(jnp.bfloat16).reshape(requests, heads, QK)
    w_key = w_up.reshape(RANK, heads, NOPE + VDIM)[:, :, :NOPE]
    dn = jnp.einsum("qhn,rhn->hqr", dq[..., :NOPE], w_key, preferred_element_type=jnp.float32)
    dr = turn(dq[..., NOPE:].astype(jnp.float32), dcos[:, None], dsin[:, None]).transpose(1, 0, 2)
    dq = (jnp.concatenate([dn, dr], -1) * SCALE).astype(jnp.bfloat16)
    own = jnp.sum(dq.astype(jnp.float32) * new_key.astype(jnp.float32)[None], -1, keepdims=True)
    per = 8 * pl.cdiv(requests, 8)
    spread = lambda v: jnp.pad(v, ((0, 0), (0, per - requests), (0, 0))).reshape(heads * per, -1)
    every = lambda v: spread(jnp.broadcast_to(v[None], (heads,) + v.shape))
    args = (
        q, latent, start[:, None], spread(dq), spread(own),
        every(new_key[:, :RANK].astype(jnp.float32)), every(starts[:, None]), every(ends[:, None]),
        page_table[:tok // PAGE] // (tok // PAGE), w_up, w_out,
    )
    vmem = pl.BlockSpec(memory_space=pltpu.VMEM)
    specs = [vmem] * len(args)
    specs[8] = pl.BlockSpec(memory_space=pltpu.SMEM)
    rows = tok // n_head
    far_count = n_head // 2 - 1
    bf = jnp.bfloat16
    out, cache, dec = pl.pallas_call(
        functools.partial(kernel, n_ctx, n_head, heads),
        out_shape=(
            jax.ShapeDtypeStruct((rows, width), bf),
            jax.ShapeDtypeStruct((tok, WIDTH), bf),
            jax.ShapeDtypeStruct((per, width), bf),
        ),
        in_specs=specs,
        out_specs=(vmem, vmem, vmem),
        scratch_shapes=[
            pltpu.VMEM((n_ctx, 2, tok // 2, WIDTH), bf),
            pltpu.VMEM((heads, tok, QK), bf),
            pltpu.VMEM((heads, tok, 2 * VDIM), bf),
            pltpu.VMEM((heads, tok, 2 * VDIM), jnp.float32),
            pltpu.VMEM((heads, tok, 128), jnp.float32),
            pltpu.VMEM((tok, heads * VDIM), bf),
        ]
        + [pltpu.VMEM((far_count, rows, width), bf)] * 4
        + [pltpu.VMEM((rows, width), bf)] * 2
        + [pltpu.VMEM((per, width), jnp.float32)] * 2
        + [pltpu.VMEM((n_head // 2, per, width), jnp.float32)]
        + [
            pltpu.SemaphoreType.DMA((5, n_ctx)),
            pltpu.SemaphoreType.DMA((n_ctx,)),
            pltpu.SemaphoreType.DMA((n_ctx,)),
            pltpu.SemaphoreType.DMA((3 * n_head // 2,)),
            pltpu.SemaphoreType.DMA((3 * n_head // 2,)),
        ],
        compiler_params=pltpu.CompilerParams(
            collective_id=0, has_side_effects=True, vmem_limit_bytes=56 * 1024 * 1024
        ),
        cost_estimate=pl.CostEstimate(
            flops=12 * 10**9, bytes_accessed=8 * 10**6, transcendentals=5 * 10**6
        ),
    )(*args)
    return out, cache, dec[:requests]


def solution(mesh):
    in_specs = (
        P("ctx", None), P(), P(), P(), P(None, "head"), P(), P(), P(None, "head"), P("head", None),
    )
    out_specs = (P(("ctx", "head"), None), P("ctx", None), P())
    return jax.shard_map(
        functools.partial(on_device, mesh.shape["ctx"], mesh.shape["head"]),
        mesh=mesh, in_specs=in_specs, out_specs=out_specs, check_vma=False,
    )
```
